256 devices in a mesh: loop: 128 (over z, y, x_lo, core), half: 2 (over x_hi).
Axes of the slice: x: 4 (x_hi: 2, x_lo: 2; x = x_hi * 2 + x_lo), y: 4, z: 8, core: 2. Of those that a mesh axis runs over, the one named last changes fastest.
Arguments:
- tokens: bfloat16 [131072, 4096], P(('loop', 'half')), may hold values from -36 to 36
- gain: float32 [4096], replicated, may hold values from 0.1 to 1.9
- w_key: bfloat16 [4096, 512], P('loop', 'half'), may hold values from -0.09375 to 0.09375
- w_value: bfloat16 [4096, 512], P('loop', 'half'), may hold values from -0.09375 to 0.09375
- d_keys: bfloat16 [131072, 512], P(('loop', 'half')), may hold values from -13.5 to 13.5
- d_values: bfloat16 [131072, 512], P(('loop', 'half')), may hold values from -13.5 to 13.5
Outputs:
- keys: bfloat16 [131072, 512], P(('loop', 'half'))
- values: bfloat16 [131072, 512], P(('loop', 'half'))
- d_tokens: bfloat16 [131072, 4096], P(('loop', 'half'))
- grad_key: float32 [4096, 512], P('loop', 'half')
- grad_value: float32 [4096, 512], P('loop', 'half')
- grad_gain: float32 [4096], replicated
The draws below stay inside these ranges and needn't reach their ends.
All inputs are finite; a program needn't handle non-finite values.
Results may differ from the reference program's by a relative error of at most 0.0049.
Values may be sent and summed in bfloat16 or wider, within the bound.
No kernel may reach another device: no remote copies, remote signals or barrier semaphores. Data moves between devices by JAX's collectives and lax.ppermute only.
A program may use at most 128 MiB of HBM per device.

```python
import math
import jax
import jax.numpy as jnp
from jax import lax

D = 4096
KVH = 4
HD = 128
TOKENS = 131072


def rising_factor(count, top):
    return 1.0 + (top - 1.0) * jnp.arange(count, dtype=jnp.float32) / max(count - 1, 1)


def log_spread(key, count, low, high):
    return jnp.exp(jax.random.uniform(key, (count,), jnp.float32, jnp.log(low), jnp.log(high)))


def draw_tokens(key, part):
    key = jax.random.fold_in(key, 11)
    first, second, third = jax.random.split(key, 3)
    base = jnp.clip(jax.random.normal(first, (TOKENS, D), jnp.float32), -4.0, 4.0)
    row_scale = log_spread(second, TOKENS, 0.3, 3.0)
    col_scale = log_spread(third, D, 0.3, 3.0)
    return (base * row_scale[:, None] * col_scale[None, :]).astype(jnp.bfloat16)


def cotangent(key):
    first = jax.random.fold_in(key, 0)
    columns = KVH * HD
    base = jnp.clip(jax.random.normal(first, (TOKENS, columns), jnp.float32), -4.5, 4.5)
    factor = rising_factor(TOKENS, 3.0)
    return (base * factor[:, None]).astype(jnp.bfloat16)


def draw_d_keys(key, part):
    key = jax.random.fold_in(key, 23)
    return cotangent(key)


def draw_d_values(key, part):
    key = jax.random.fold_in(key, 37)
    return cotangent(key)


def block_scale(stream_key, dims, cuts, low, largest):
    loudness, own = 1.0, jax.random.fold_in(stream_key, 6)
    for dim, blocks in cuts:
        heights = jnp.exp(jax.random.uniform(jax.random.fold_in(own, dim), (blocks,), jnp.float32, low / len(cuts), largest / len(cuts)))
        loudness = loudness * jnp.repeat(heights, dims[dim] // blocks).reshape([-1 if axis == dim else 1 for axis in range(len(dims))])
    return loudness


def scatter_about(own_key, dims, deviation, bound, shards=(), held_as=jnp.bfloat16):
    loudness = block_scale(own_key, dims, shards, -0.22, 0.18) if shards else 1.0
    entries = jax.random.normal(own_key, dims, jnp.float32) * deviation * loudness
    return jnp.minimum(jnp.maximum(entries, -bound), bound).astype(held_as)


def setup_inputs(seed: int = 0) -> dict:
    streams_of = jax.random.split(jax.random.key(seed), 7)
    return {
        "tokens": draw_tokens(jax.random.fold_in(streams_of[6], 71), 0),
        "gain": jnp.clip(1.0 + 0.18 * jax.random.normal(streams_of[1], (D,), jnp.float32), 0.1, 1.9),
        "w_key": scatter_about(streams_of[2], (D, KVH * HD), D ** -0.5, 0.09375, ((0, 128), (1, 2))),
        "w_value": scatter_about(streams_of[3], (D, KVH * HD), D ** -0.5, 0.09375, ((0, 128), (1, 2))),
        "d_keys": draw_d_keys(jax.random.fold_in(streams_of[6], 71), 0),
        "d_values": draw_d_values(jax.random.fold_in(streams_of[6], 71), 0),
    }


def reference(tokens, gain, w_key, w_value, d_keys, d_values):
    block = math.gcd(TOKENS, 2048)
    count = TOKENS // block
    scale = 1.0 / math.sqrt(TOKENS)

    def one_block(carry, items):
        tok_rows, key_cot, value_cot = items
        x_rows = tok_rows.astype(jnp.float32)
        inverse = lax.rsqrt(lax.optimization_barrier(jnp.mean(x_rows * x_rows, axis=1, keepdims=True)) + 1e-05)
        normal_rows = x_rows * inverse
        hidden = (normal_rows * gain).astype(jnp.bfloat16)
        key_rows = jnp.dot(hidden, w_key, preferred_element_type=jnp.float32).astype(jnp.bfloat16)
        value_rows = jnp.dot(hidden, w_value, preferred_element_type=jnp.float32).astype(jnp.bfloat16)
        grad_k, grad_v, grad_g = carry
        grad_k = grad_k + jnp.dot(hidden.T, key_cot, preferred_element_type=jnp.float32)
        grad_v = grad_v + jnp.dot(hidden.T, value_cot, preferred_element_type=jnp.float32)
        d_hidden = jnp.dot(key_cot, w_key.T, preferred_element_type=jnp.float32)
        d_hidden = d_hidden + jnp.dot(value_cot, w_value.T, preferred_element_type=jnp.float32)
        grad_g = grad_g + lax.optimization_barrier(jnp.sum(d_hidden * normal_rows, axis=0))
        scaled = d_hidden * gain
        along = lax.optimization_barrier(jnp.mean(scaled * normal_rows, axis=1, keepdims=True))
        d_rows = (inverse * (scaled - normal_rows * along)).astype(jnp.bfloat16)
        return ((grad_k, grad_v, grad_g), (key_rows, value_rows, d_rows))
    columns = KVH * HD
    stacks = (tokens.reshape(count, block, D), d_keys.reshape(count, block, columns), d_values.reshape(count, block, columns))
    init = (jnp.zeros((D, columns), jnp.float32), jnp.zeros((D, columns), jnp.float32), jnp.zeros((D,), jnp.float32))
    (grad_k, grad_v, grad_g), (keys, values, d_tokens) = lax.scan(one_block, init, stacks)
    return (keys.reshape(TOKENS, columns), values.reshape(TOKENS, columns), d_tokens.reshape(TOKENS, D), grad_k * scale, grad_v * scale, grad_g * scale)
```

```python
import math

import jax
import jax.numpy as jnp
from jax import lax
from jax.experimental import pallas as pl
from jax.experimental.pallas import tpu as pltpu
from jax.sharding import Mesh
from jax.sharding import PartitionSpec as P

Z, Y, XL, CORE, XH = 8, 4, 2, 2, 2
AXES = ("z", "y", "xl", "core", "xh")
PLANE = ("y", "xl", "xh")
ROWS = 512
D = 4096
C = 512
W = D // Z
HALF = C // XH
BLOCK = 32
EPS = 1e-05
BF = jnp.bfloat16
F32 = jnp.float32
VMEM = 44 * 1024 * 1024


def inverse_of(x):
    x = x.astype(F32)
    return lax.rsqrt(jnp.sum(x * x, axis=1, keepdims=True) * (1.0 / D) + EPS)


def grads_kernel(own_ref, other_ref, gain_ref, d_own_ref, d_other_ref, out_ref, inv_ref):
    step = pl.program_id(0)

    @pl.when(step == 0)
    def _():
        inv_ref[0] = jnp.broadcast_to(inverse_of(own_ref[...]), (ROWS, 128))
        inv_ref[1] = jnp.broadcast_to(inverse_of(other_ref[...]), (ROWS, 128))

    columns = pl.ds(pl.multiple_of(step * W, W), W)
    gain = gain_ref[:, columns]

    def term(x_ref, which, d_ref):
        normal = x_ref[:, columns].astype(F32) * inv_ref[which, :, :1]
        hidden = (normal * gain).astype(BF)
        return lax.dot_general(
            hidden, d_ref[...], (((0,), (0,)), ((), ())), preferred_element_type=F32
        )

    total = term(own_ref, 0, d_own_ref) + term(other_ref, 1, d_other_ref)
    total = total.astype(BF)
    for place in range(Y * XL):
        for core in range(CORE):
            for half in range(XH):
                first = (place * CORE + core) * BLOCK
                out_ref[place * XH + half, 0, core] = total[
                    first : first + BLOCK, half * HALF : (half + 1) * HALF
                ]


def gradient_terms(own, other, gain, d_own, d_other):
    whole = lambda shape: pl.BlockSpec(shape, lambda i: (0,) * len(shape))
    return pl.pallas_call(
        grads_kernel,
        grid=(Z,),
        in_specs=[
            whole((ROWS, D)),
            whole((ROWS, D)),
            whole((1, D)),
            whole((ROWS, C)),
            whole((ROWS, C)),
        ],
        out_specs=pl.BlockSpec((Y * XL * XH, 1, CORE, BLOCK, HALF), lambda i: (0, i, 0, 0, 0)),
        out_shape=jax.ShapeDtypeStruct((Y * XL * XH, Z, CORE, BLOCK, HALF), BF),
        scratch_shapes=[pltpu.VMEM((2, ROWS, 128), F32)],
        compiler_params=pltpu.CompilerParams(vmem_limit_bytes=VMEM),
        cost_estimate=pl.CostEstimate(
            flops=2 * 2 * ROWS * D * C, bytes_accessed=13 << 20, transcendentals=2 * ROWS
        ),
        name="gradient_terms",
    )(own, other, gain, d_own, d_other)


def rows_kernel(x_ref, gain_ref, d0_ref, d1_ref, w0_ref, w1_ref, out0_ref, out1_ref, dx_ref,
                inv_ref, total_ref, along_ref):
    step = pl.program_id(0)

    @pl.when(step == 0)
    def _():
        inv_ref[...] = jnp.broadcast_to(inverse_of(x_ref[...]), (ROWS, 128))
        total_ref[...] = jnp.zeros_like(total_ref)

    columns = pl.ds(pl.multiple_of(lax.rem(step, Z) * W, W), W)
    gain = gain_ref[:, columns]
    normal = x_ref[:, columns].astype(F32) * inv_ref[:, :1]
    weights = jnp.concatenate(
        [ref[:, half].reshape(W, HALF) for ref in (w0_ref, w1_ref) for half in range(XH)], axis=1
    )

    @pl.when(step < Z)
    def _():
        hidden = (normal * gain).astype(BF)
        total_ref[...] += jnp.dot(hidden, weights, preferred_element_type=F32)

    @pl.when(step == Z)
    def _():
        first, second = total_ref[:, :C], total_ref[:, C:]
        along = jnp.sum(
            first * d0_ref[...].astype(F32) + second * d1_ref[...].astype(F32),
            axis=1,
            keepdims=True,
        )
        along_ref[...] = jnp.broadcast_to(along * (1.0 / D), (ROWS, 128))
        out0_ref[...] = first.astype(BF)
        out1_ref[...] = second.astype(BF)

    @pl.when(step >= Z)
    def _():
        cotangents = jnp.concatenate([d0_ref[...], d1_ref[...]], axis=1)
        d_hidden = lax.dot_general(
            cotangents, weights, (((1,), (1,)), ((), ())), preferred_element_type=F32
        )
        inverse = inv_ref[:, :1]
        dx_ref[...] = (inverse * (d_hidden * gain - normal * along_ref[:, :1])).astype(BF)


def rows_pass(x, gain, d0, d1, w0, w1):
    whole = lambda shape: pl.BlockSpec(shape, lambda i: (0,) * len(shape))
    weights = pl.BlockSpec((D // BLOCK // Z, XH, BLOCK, HALF), lambda i: (lax.rem(i, Z), 0, 0, 0))
    return pl.pallas_call(
        rows_kernel,
        grid=(2 * Z,),
        in_specs=[
            whole((ROWS, D)),
            whole((1, D)),
            whole((ROWS, C)),
            whole((ROWS, C)),
            weights,
            weights,
        ],
        out_specs=[
            whole((ROWS, C)),
            whole((ROWS, C)),
            pl.BlockSpec((ROWS, W), lambda i: (0, jnp.maximum(i - Z, 0))),
        ],
        out_shape=[
            jax.ShapeDtypeStruct((ROWS, C), BF),
            jax.ShapeDtypeStruct((ROWS, C), BF),
            jax.ShapeDtypeStruct((ROWS, D), BF),
        ],
        scratch_shapes=[
            pltpu.VMEM((ROWS, 128), F32),
            pltpu.VMEM((ROWS, 2 * C), F32),
            pltpu.VMEM((ROWS, 128), F32),
        ],
        compiler_params=pltpu.CompilerParams(vmem_limit_bytes=VMEM),
        cost_estimate=pl.CostEstimate(
            flops=2 * 2 * ROWS * D * 2 * C, bytes_accessed=26 << 20, transcendentals=ROWS
        ),
        name="rows_pass",
    )(x, gain, d0, d1, w0, w1)


def shards(tokens, gain, w_key, w_value, d_keys, d_values):
    scale = 1.0 / math.sqrt(ROWS * Z * Y * XL * CORE * XH)
    core = lax.axis_index("core")
    swap = lambda a: lax.ppermute(a, "core", [(0, 1), (1, 0)])
    row_gain = gain.reshape(1, D)

    pair = jnp.stack([w_key, w_value])
    sent = jnp.broadcast_to(pair[None, :, None], (Y * XL, CORE, XH, BLOCK, HALF))
    plane = lax.all_to_all(
        sent.reshape(Y * XL * CORE * XH, BLOCK, HALF), ("y", "xl", "core", "xh"), 0, 0, tiled=True
    )
    mine = lax.all_gather(plane, "z", axis=0, tiled=True)
    mine = mine.reshape(D // BLOCK, XH, BLOCK, HALF)
    theirs = swap(mine)

    first = core == 0
    d_mine = jnp.where(first, d_keys, d_values)
    d_theirs = jnp.where(first, d_values, d_keys)
    terms = gradient_terms(tokens, swap(tokens), row_gain, d_mine, swap(d_theirs))
    summed = lax.all_to_all(terms, PLANE, 0, 0, tiled=True)
    summed = jnp.sum(summed.astype(F32), axis=0)

    place = lax.axis_index("y") * XL + lax.axis_index("xl")
    blocks = mine.reshape(Z, Y * XL, CORE, XH, BLOCK, HALF)
    blocks = lax.dynamic_slice(
        blocks,
        (0, place, 0, lax.axis_index("xh"), 0, 0),
        (Z, 1, CORE, 1, BLOCK, HALF),
    ).reshape(Z, CORE, BLOCK, HALF)
    gains = jnp.sum(summed * blocks.astype(F32), axis=3).reshape(2, HALF)
    high = gains.astype(BF)
    low = (gains - high.astype(F32)).astype(BF)
    extra = jnp.concatenate([high, low, jnp.zeros((12, HALF), BF)])
    sent = jnp.concatenate(
        [
            summed.astype(BF).reshape(Z * CORE, BLOCK, HALF),
            jnp.broadcast_to(extra[None], (Z * CORE, 16, HALF)),
        ],
        axis=1,
    )
    received = lax.all_to_all(sent, ("z", "core"), 0, 0, tiled=True).astype(F32)
    grads = jnp.sum(received[:, :BLOCK].reshape(Z, 2, BLOCK, HALF), axis=0) * scale
    gains = jnp.sum(received[:, BLOCK : BLOCK + 4], axis=0)
    gains = (gains[:2] + gains[2:]).reshape(1, 4, 128)
    gains = lax.all_to_all(
        jnp.broadcast_to(gains, (Y * XL * XH, 4, 128)), PLANE, 0, 0, tiled=True
    )
    gains = jnp.sum(gains.reshape(Y * XL, XH, Z, CORE * BLOCK), axis=1)
    grad_gain = jnp.transpose(gains, (1, 0, 2)).reshape(D) * scale / gain

    out_mine, out_theirs, d_tokens = rows_pass(tokens, row_gain, d_mine, d_theirs, mine, theirs)
    keys = jnp.where(first, out_mine, out_theirs)
    values = jnp.where(first, out_theirs, out_mine)
    return (keys, values, d_tokens, grads[0], grads[1], grad_gain)


def solution(mesh):
    fine = Mesh(mesh.devices.reshape(Z, Y, XL, CORE, XH), AXES)
    loop = ("z", "y", "xl", "core")
    return jax.shard_map(
        shards,
        mesh=fine,
        in_specs=(
            P(AXES, None),
            P(),
            P(loop, "xh"),
            P(loop, "xh"),
            P(AXES, None),
            P(AXES, None),
        ),
        out_specs=(
            P(AXES, None),
            P(AXES, None),
            P(AXES, None),
            P(loop, "xh"),
            P(loop, "xh"),
            P(),
        ),
        check_vma=False,
    )
```

```python
import math

import jax
import jax.numpy as jnp
from jax import lax
from jax.experimental import pallas as pl
from jax.experimental.pallas import tpu as pltpu
from jax.sharding import Mesh
from jax.sharding import PartitionSpec as P

Z, Y, XL, CORE, XH = 8, 4, 2, 2, 2
X = XL * XH
AXES = ("z", "y", "xl", "core", "xh")
PLANE = ("y", "xl", "xh")
ROWS = 512
D = 4096
C = 512
W = D // Z
HALF = C // XH
BLOCK = 32
PART = Z // 2
EPS = 1e-05
BF = jnp.bfloat16
F32 = jnp.float32
VMEM = 60 * 1024 * 1024
SMALL = 8 * 1024 * 1024


def params(limit=VMEM):
    return pltpu.CompilerParams(vmem_limit_bytes=limit)


def tie_kernel(a_ref, other_ref, out_ref):
    del a_ref, other_ref, out_ref


def after(a, other):
    return pl.pallas_call(
        tie_kernel,
        in_specs=[pl.BlockSpec(memory_space=pl.ANY)] * 2,
        out_specs=pl.BlockSpec(memory_space=pl.ANY),
        out_shape=jax.ShapeDtypeStruct(a.shape, a.dtype),
        input_output_aliases={0: 0},
        name="after",
    )(a, other)


def copies(pairs, sems):
    started = []
    for at, (source, target) in enumerate(pairs):
        copy = pltpu.make_async_copy(source, target, sems.at[at])
        copy.start()
        started.append(copy)
    return started


def pick(core, first, second, target, sem):
    @pl.when(core == 0)
    def _():
        pltpu.make_async_copy(first, target, sem).start()

    @pl.when(core != 0)
    def _():
        pltpu.make_async_copy(second, target, sem).start()

    return pltpu.make_async_copy(first, target, sem)


SMEM = pl.BlockSpec(memory_space=pltpu.SMEM)
ANY = pl.BlockSpec(memory_space=pl.ANY)
INNER = pl.BlockSpec(memory_space=pltpu.VMEM)


def cheap():
    return pl.CostEstimate(flops=1 << 20, bytes_accessed=1 << 20, transcendentals=0)


def inverse_kernel(x_ref, out_ref, x_buf, sems):
    rows = ROWS // 8
    parts = [pl.ds(i * rows, rows) for i in range(8)]
    started = copies([(x_ref.at[part], x_buf.at[part]) for part in parts], sems)
    for part, copy in zip(parts, started):
        copy.wait()
        squares = jnp.zeros((rows, 128), F32)
        for j in range(D // 128):
            piece = x_buf[part, j * 128 : (j + 1) * 128].astype(F32)
            squares = squares + piece * piece
        mean = jnp.sum(squares, axis=1, keepdims=True) * (1.0 / D)
        out_ref[part, :] = jnp.broadcast_to(lax.rsqrt(mean + EPS), (rows, 128))


def inverses(x):
    return pl.pallas_call(
        inverse_kernel,
        in_specs=[ANY],
        out_specs=INNER,
        out_shape=jax.ShapeDtypeStruct((ROWS, 128), F32),
        scratch_shapes=[pltpu.VMEM((ROWS, D), BF), pltpu.SemaphoreType.DMA((8,))],
        compiler_params=params(),
        cost_estimate=cheap(),
        name="inverses",
    )(x)


WIDE = 2 * W


def grads_kernel(along_x, place_ref, own_ref, other_ref, gain_ref, inv_own_ref, inv_other_ref,
                 keys_own_ref, values_own_ref, keys_other_ref, values_other_ref, *rest):
    outs = rest[:4]
    x_buf, d_buf, inv_buf, gain_buf, total_ref, out_buf, sems, out_sems = rest[4:]
    x_at, y_at, core_at = place_ref[0], place_ref[1], place_ref[2]
    start = 0 if along_x else PART * W
    parts = PART * W // WIDE
    small = copies(
        [
            (gain_ref.at[:, pl.ds(start, PART * W)], gain_buf),
            (inv_own_ref, inv_buf.at[0]),
            (inv_other_ref, inv_buf.at[1]),
        ],
        sems,
    )
    small.append(pick(core_at, keys_own_ref, values_own_ref, d_buf.at[0], sems.at[3]))
    small.append(pick(core_at, keys_other_ref, values_other_ref, d_buf.at[1], sems.at[4]))
    large = []
    for part in range(parts):
        for which, ref in enumerate((own_ref, other_ref)):
            for piece in range(2):
                lanes = pl.ds(part * WIDE + piece * W, W)
                copy = pltpu.make_async_copy(
                    ref.at[:, pl.ds(start + part * WIDE + piece * W, W)],
                    x_buf.at[which, :, lanes],
                    sems.at[5 + len(large)],
                )
                copy.start()
                large.append(copy)
    for copy in small:
        copy.wait()
    sent = []
    for part in range(parts):
        for copy in large[4 * part : 4 * part + 4]:
            copy.wait()
        lanes = slice(part * WIDE, (part + 1) * WIDE)
        total = None
        for which in range(2):
            normal = x_buf[which, :, lanes].astype(F32) * inv_buf[which, :, :1]
            hidden = (normal * gain_buf[:, lanes]).astype(BF)
            term = lax.dot_general(
                hidden, d_buf[which], (((0,), (0,)), ((), ())), preferred_element_type=F32
            )
            total = term if total is None else total + term
        total_ref[lanes, :] = total.astype(BF)
        for z in range(part * WIDE // W, (part + 1) * WIDE // W):
            for shift in range(4):
                for other in range(4):
                    if along_x:
                        x, y = lax.rem(x_at + shift, X), other
                    else:
                        x, y = other, lax.rem(y_at + shift, Y)
                    low, high = lax.rem(x, XL), lax.div(x, XL)
                    columns = pl.ds(pl.multiple_of(high * HALF, HALF), HALF)
                    for core in range(CORE):
                        first = z * W + ((y * XL + low) * CORE + core) * BLOCK
                        first = pl.multiple_of(first, BLOCK)
                        out_buf[shift, other, z, core] = total_ref[pl.ds(first, BLOCK), columns]
        zs = pl.ds(part * WIDE // W, WIDE // W)
        for shift in range(4):
            copy = pltpu.make_async_copy(
                out_buf.at[shift, :, zs], outs[shift].at[:, zs], out_sems.at[part, shift]
            )
            copy.start()
            sent.append(copy)
    for copy in sent:
        copy.wait()


def gradient_terms(toward_x, *inputs):
    shape = (4, PART, CORE, BLOCK, HALF)

    def kernel(*refs):
        grads_kernel(toward_x, *refs)

    return pl.pallas_call(
        kernel,
        in_specs=[SMEM] + [ANY] * 9,
        out_specs=[ANY] * 4,
        out_shape=[jax.ShapeDtypeStruct(shape, BF)] * 4,
        scratch_shapes=[
            pltpu.VMEM((2, ROWS, PART * W), BF),
            pltpu.VMEM((2, ROWS, C), BF),
            pltpu.VMEM((2, ROWS, 128), F32),
            pltpu.VMEM((1, PART * W), F32),
            pltpu.VMEM((PART * W, C), BF),
            pltpu.VMEM((4,) + shape, BF),
            pltpu.SemaphoreType.DMA((13,)),
            pltpu.SemaphoreType.DMA((2, 4)),
        ],
        compiler_params=params(),
        cost_estimate=pl.CostEstimate(
            flops=2 * ROWS * D * C, bytes_accessed=8 << 20, transcendentals=0
        )
        if toward_x
        else cheap(),
        name="gradient_terms_x" if toward_x else "gradient_terms_y",
    )(*inputs)


def sums_kernel(place_ref, *refs):
    ins, outs = refs[:4], refs[4:]
    for shift in range(4):
        at = lax.rem(place_ref[0] + shift, 4)
        total = ins[0][at].astype(F32)
        for ref in ins[1:]:
            total = total + ref[at].astype(F32)
        outs[shift][...] = total.astype(outs[shift].dtype)


def sums(at, pieces, name):
    shape = (PART, CORE, BLOCK, HALF)
    return pl.pallas_call(
        sums_kernel,
        in_specs=[SMEM] + [INNER] * 4,
        out_specs=[INNER] * 4,
        out_shape=[jax.ShapeDtypeStruct(shape, F32 if k == 0 else BF) for k in range(4)],
        compiler_params=params(SMALL),
        cost_estimate=pl.CostEstimate(flops=1 << 20, bytes_accessed=3 << 20, transcendentals=0),
        name=name,
    )(at.reshape(1), *pieces)


EXTRA = 16


def pack_kernel(*refs):
    x_first, y_first, w_ref, out_ref, prod_ref = refs[:4], refs[4:8], refs[8], refs[9], refs[10]
    for start, pieces in ((0, x_first), (PART, y_first)):
        for z in range(PART):
            for core in range(CORE):
                total = pieces[0][z, core]
                for ref in pieces[1:]:
                    total = total + ref[z, core].astype(F32)
                at = (start + z) * CORE + core
                out_ref[at, :BLOCK] = total.astype(BF)
                prod_ref[at * BLOCK : (at + 1) * BLOCK] = total * w_ref[at].astype(F32)
    gains = lax.dot_general(
        jnp.ones((8, HALF), F32),
        prod_ref[...],
        (((1,), (1,)), ((), ())),
        precision=lax.Precision.HIGHEST,
        preferred_element_type=F32,
    )[:1]
    upper = gains.astype(BF).astype(F32)
    lower = gains - upper
    row = lax.broadcasted_iota(jnp.int32, (EXTRA, HALF), 0)
    extra = jnp.zeros((EXTRA, HALF), F32)
    for at, line in enumerate(
        (upper[:, :HALF], upper[:, HALF:], lower[:, :HALF], lower[:, HALF:])
    ):
        extra = jnp.where(row == at, jnp.broadcast_to(line, (EXTRA, HALF)), extra)
    extra = extra.astype(BF)
    for at in range(Z * CORE):
        out_ref[at, BLOCK:] = extra


def pack(x_first, y_first, blocks):
    return pl.pallas_call(
        pack_kernel,
        in_specs=[INNER] * 9,
        out_specs=INNER,
        out_shape=jax.ShapeDtypeStruct((Z * CORE, BLOCK + EXTRA, HALF), BF),
        scratch_shapes=[pltpu.VMEM((Z * CORE * BLOCK, HALF), F32)],
        compiler_params=params(SMALL),
        cost_estimate=cheap(),
        name="pack",
    )(*x_first, *y_first, blocks)


def unpack_kernel(scale, in_ref, key_ref, value_ref, gains_ref):
    for which, ref in enumerate((key_ref, value_ref)):
        total = in_ref[which, :BLOCK].astype(F32)
        for z in range(1, Z):
            total = total + in_ref[z * 2 + which, :BLOCK].astype(F32)
        ref[...] = total * scale
    extra = in_ref[0, BLOCK:].astype(F32)
    for at in range(1, Z * CORE):
        extra = extra + in_ref[at, BLOCK:].astype(F32)
    for line in range(2):
        gains = extra[line : line + 1] + extra[line + 2 : line + 3]
        for piece in range(2):
            lanes = gains[:, piece * 128 : (piece + 1) * 128]
            for at in range(Y * XL * XH):
                gains_ref[at, line * 2 + piece : line * 2 + piece + 1] = lanes


def unpack(scale, received):
    def kernel(*refs):
        unpack_kernel(scale, *refs)

    return pl.pallas_call(
        kernel,
        in_specs=[INNER],
        out_specs=[INNER] * 3,
        out_shape=[
            jax.ShapeDtypeStruct((BLOCK, HALF), F32),
            jax.ShapeDtypeStruct((BLOCK, HALF), F32),
            jax.ShapeDtypeStruct((Y * XL * XH, 4, 128), F32),
        ],
        compiler_params=params(SMALL),
        cost_estimate=cheap(),
        name="unpack",
    )(received)


STEPS = D // WIDE


def weight_rows(buf, part):
    rows = WIDE // BLOCK
    ref = buf.at[pl.ds(part * rows, rows)]
    return jnp.concatenate([ref[:, half].reshape(WIDE, HALF) for half in range(XH)], axis=1)


def hidden_columns(x_buf, inv_buf, gain_buf, part):
    lanes = slice(part * WIDE, (part + 1) * WIDE)
    return (x_buf[:, lanes].astype(F32) * inv_buf[:, :1] * gain_buf[:, lanes]).astype(BF)


def pieces_of(x_ref, x_buf, weights):
    pairs = []
    rows = D // BLOCK // Z
    for part in range(STEPS):
        for at in range(part * WIDE // W, (part + 1) * WIDE // W):
            lanes = pl.ds(at * W, W)
            pairs.append((x_ref.at[:, lanes], x_buf.at[:, lanes]))
            for ref, buf in weights:
                block = pl.ds(at * rows, rows)
                pairs.append((ref.at[block], buf.at[block]))
    return pairs


def forward_kernel(place_ref, x_ref, gain_ref, inv_ref, keys_ref, values_ref, w_ref,
                   out_ref, along_ref, x_buf, w_buf, d_buf, inv_buf, gain_buf, sems, small_sems):
    small = copies([(gain_ref, gain_buf), (inv_ref, inv_buf)], small_sems)
    small.append(pick(place_ref[2], keys_ref, values_ref, d_buf, small_sems.at[2]))
    large = copies(pieces_of(x_ref, x_buf, [(w_ref, w_buf)]), sems)
    each = len(large) // STEPS
    for copy in small:
        copy.wait()
    total = None
    for part in range(STEPS):
        for copy in large[part * each : (part + 1) * each]:
            copy.wait()
        hidden = hidden_columns(x_buf, inv_buf, gain_buf, part)
        term = jnp.dot(hidden, weight_rows(w_buf, part), preferred_element_type=F32)
        total = term if total is None else total + term
    out_ref[...] = total.astype(BF)
    along = jnp.sum(total * d_buf[...].astype(F32), axis=1, keepdims=True) * (1.0 / D)
    along_ref[...] = jnp.broadcast_to(along, (ROWS, 128))


def forward(*inputs):
    return pl.pallas_call(
        forward_kernel,
        in_specs=[SMEM] + [ANY] * 6,
        out_specs=[INNER] * 2,
        out_shape=[
            jax.ShapeDtypeStruct((ROWS, C), BF),
            jax.ShapeDtypeStruct((ROWS, 128), F32),
        ],
        scratch_shapes=[
            pltpu.VMEM((ROWS, D), BF),
            pltpu.VMEM((D // BLOCK, XH, BLOCK, HALF), BF),
            pltpu.VMEM((ROWS, C), BF),
            pltpu.VMEM((ROWS, 128), F32),
            pltpu.VMEM((1, D), F32),
            pltpu.SemaphoreType.DMA((16,)),
            pltpu.SemaphoreType.DMA((3,)),
        ],
        compiler_params=params(),
        cost_estimate=cheap(),
        name="forward",
    )(*inputs)


def backward_kernel(place_ref, x_ref, gain_ref, inv_ref, keys_ref, values_ref, mine_ref,
                    theirs_ref, done_ref, along_ref, out_keys_ref, out_values_ref, dx_ref,
                    x_buf, mine_buf, theirs_buf, d_buf, inv_buf, gain_buf, along_buf, out_buf,
                    dx_buf, sems, small_sems, out_sems, dx_sems):
    core = place_ref[2]
    small = copies(
        [(gain_ref, gain_buf), (inv_ref, inv_buf), (along_ref, along_buf), (done_ref, out_buf.at[0])],
        small_sems,
    )
    small.append(pick(core, keys_ref, values_ref, d_buf.at[0], small_sems.at[4]))
    small.append(pick(core, values_ref, keys_ref, d_buf.at[1], small_sems.at[5]))
    large = copies(
        pieces_of(x_ref, x_buf, [(theirs_ref, theirs_buf), (mine_ref, mine_buf)]), sems
    )
    each = len(large) // STEPS
    for copy in small:
        copy.wait()
    total = None
    for part in range(STEPS):
        for copy in large[part * each : (part + 1) * each]:
            copy.wait()
        hidden = hidden_columns(x_buf, inv_buf, gain_buf, part)
        term = jnp.dot(hidden, weight_rows(theirs_buf, part), preferred_element_type=F32)
        total = term if total is None else total + term
    out_buf[1] = total.astype(BF)
    sent = []
    for which in range(2):
        refs = (out_keys_ref, out_values_ref) if which == 0 else (out_values_ref, out_keys_ref)

        @pl.when(core == 0)
        def _():
            pltpu.make_async_copy(out_buf.at[which], refs[0], out_sems.at[which]).start()

        @pl.when(core != 0)
        def _():
            pltpu.make_async_copy(out_buf.at[which], refs[1], out_sems.at[which]).start()

        sent.append(pltpu.make_async_copy(out_buf.at[which], refs[0], out_sems.at[which]))
    along = jnp.sum(total * d_buf[1].astype(F32), axis=1, keepdims=True) * (1.0 / D)
    along = along + along_buf[:, :1]
    inverse = inv_buf[:, :1]
    for part in range(STEPS):
        lanes = slice(part * WIDE, (part + 1) * WIDE)
        d_hidden = None
        for which, buf in enumerate((mine_buf, theirs_buf)):
            term = lax.dot_general(
                d_buf[which],
                weight_rows(buf, part),
                (((1,), (1,)), ((), ())),
                preferred_element_type=F32,
            )
            d_hidden = term if d_hidden is None else d_hidden + term
        normal = x_buf[:, lanes].astype(F32) * inverse
        dx_buf[:, lanes] = (inverse * (d_hidden * gain_buf[:, lanes] - normal * along)).astype(BF)
        span = pl.ds(part * WIDE, WIDE)
        copy = pltpu.make_async_copy(dx_buf.at[:, span], dx_ref.at[:, span], dx_sems.at[part])
        copy.start()
        sent.append(copy)
    for copy in sent:
        copy.wait()


def backward(*inputs):
    return pl.pallas_call(
        backward_kernel,
        in_specs=[SMEM] + [ANY] * 9,
        out_specs=[ANY] * 3,
        out_shape=[
            jax.ShapeDtypeStruct((ROWS, C), BF),
            jax.ShapeDtypeStruct((ROWS, C), BF),
            jax.ShapeDtypeStruct((ROWS, D), BF),
        ],
        scratch_shapes=[
            pltpu.VMEM((ROWS, D), BF),
            pltpu.VMEM((D // BLOCK, XH, BLOCK, HALF), BF),
            pltpu.VMEM((D // BLOCK, XH, BLOCK, HALF), BF),
            pltpu.VMEM((2, ROWS, C), BF),
            pltpu.VMEM((ROWS, 128), F32),
            pltpu.VMEM((1, D), F32),
            pltpu.VMEM((ROWS, 128), F32),
            pltpu.VMEM((2, ROWS, C), BF),
            pltpu.VMEM((ROWS, D), BF),
            pltpu.SemaphoreType.DMA((24,)),
            pltpu.SemaphoreType.DMA((6,)),
            pltpu.SemaphoreType.DMA((2,)),
            pltpu.SemaphoreType.DMA((STEPS,)),
        ],
        compiler_params=params(),
        cost_estimate=pl.CostEstimate(
            flops=6 * ROWS * D * C, bytes_accessed=18 << 20, transcendentals=0
        ),
        name="backward",
    )(*inputs)


def swap(a):
    return lax.ppermute(a, "core", [(0, 1), (1, 0)])


def x_index(at):
    return (at % XL) * XH + at // XL


def along_x(a, shift):
    pairs = [(x_index(i), x_index((i + shift) % X)) for i in range(X)]
    return lax.ppermute(a, ("xl", "xh"), pairs)


def along_y(a, shift):
    return lax.ppermute(a, "y", [(i, (i + shift) % Y) for i in range(Y)])


def spread(move, pieces):
    return [pieces[0]] + [move(pieces[shift], shift) for shift in range(1, 4)]


def shards(tokens, gain, w_key, w_value, d_keys, d_values):
    scale = 1.0 / math.sqrt(ROWS * Z * Y * XL * CORE * XH)
    y_at, low, high = lax.axis_index("y"), lax.axis_index("xl"), lax.axis_index("xh")
    x_at = high * XL + low
    place = jnp.stack([x_at, y_at, lax.axis_index("core")]).astype(jnp.int32)
    row_gain = gain.reshape(1, D)

    pair = jnp.stack([w_key, w_value])
    sent = jnp.broadcast_to(pair[None, :, None], (Y * XL, CORE, XH, BLOCK, HALF))
    plane = lax.all_to_all(
        sent.reshape(Y * XL * CORE * XH, BLOCK, HALF), ("y", "xl", "core", "xh"), 0, 0, tiled=True
    )

    inv = inverses(tokens)
    inputs = (place, tokens, swap(tokens), row_gain, inv, swap(inv))
    inputs += (d_keys, d_values, swap(d_keys), swap(d_values))
    y_first = gradient_terms(False, *inputs)
    x_first = gradient_terms(True, *inputs)
    plane = after(plane, y_first[0])
    mine = lax.all_gather(plane, "z", axis=0, tiled=True)

    x_first = spread(along_y, sums(place[1], spread(along_x, x_first), "sums_x"))
    y_first = spread(along_x, sums(place[0], spread(along_y, y_first), "sums_y"))
    blocks = lax.dynamic_slice(
        mine.reshape(Z, Y * XL, CORE, XH, BLOCK, HALF),
        (0, y_at * XL + low, 0, high, 0, 0),
        (Z, 1, CORE, 1, BLOCK, HALF),
    ).reshape(Z * CORE, BLOCK, HALF)
    sent = pack(x_first, y_first, blocks)
    received = lax.all_to_all(sent, ("z", "core"), 0, 0, tiled=True)

    mine = after(mine, sent).reshape(D // BLOCK, XH, BLOCK, HALF)
    theirs = swap(mine)
    row_inputs = (place, tokens, row_gain, inv, d_keys, d_values, mine)
    out_mine, along = forward(*row_inputs)
    grad_key, grad_value, gains = unpack(scale, after(received, along))

    keys, values, d_tokens = backward(*row_inputs, theirs, out_mine, along)
    gains = lax.all_to_all(gains, PLANE, 0, 0, tiled=True)
    gains = after(gains, d_tokens)
    gains = jnp.sum(gains.reshape(Y * XL, XH, Z, CORE * BLOCK), axis=1)
    grad_gain = jnp.transpose(gains, (1, 0, 2)).reshape(D) * scale / gain
    return (keys, values, d_tokens, grad_key, grad_value, grad_gain)


def solution(mesh):
    fine = Mesh(mesh.devices.reshape(Z, Y, XL, CORE, XH), AXES)
    loop = ("z", "y", "xl", "core")
    return jax.shard_map(
        shards,
        mesh=fine,
        in_specs=(
            P(AXES, None),
            P(),
            P(loop, "xh"),
            P(loop, "xh"),
            P(AXES, None),
            P(AXES, None),
        ),
        out_specs=(
            P(AXES, None),
            P(AXES, None),
            P(AXES, None),
            P(loop, "xh"),
            P(loop, "xh"),
            P(),
        ),
        check_vma=False,
    )
```

```python
import math

import jax
import jax.numpy as jnp
from jax import lax
from jax.experimental import pallas as pl
from jax.experimental.pallas import tpu as pltpu
from jax.sharding import Mesh
from jax.sharding import PartitionSpec as P

Z, Y, XL, CORE, XH = 8, 4, 2, 2, 2
AXES = ("z", "y", "xl", "core", "xh")
PLANE = ("y", "xl", "xh")
ROWS = 512
D = 4096
C = 512
W = D // Z
HALF = C // XH
BLOCK = 32
EPS = 1e-05
BF = jnp.bfloat16
F32 = jnp.float32
VMEM = 60 * 1024 * 1024
SMALL = 8 * 1024 * 1024


def params(limit=VMEM):
    return pltpu.CompilerParams(vmem_limit_bytes=limit)


def tie_kernel(a_ref, other_ref, out_ref):
    del a_ref, other_ref, out_ref


def after(a, other):
    return pl.pallas_call(
        tie_kernel,
        in_specs=[pl.BlockSpec(memory_space=pl.ANY)] * 2,
        out_specs=pl.BlockSpec(memory_space=pl.ANY),
        out_shape=jax.ShapeDtypeStruct(a.shape, a.dtype),
        input_output_aliases={0: 0},
        cost_estimate=pl.CostEstimate(flops=0, bytes_accessed=0, transcendentals=0),
        name="after",
    )(a, other)


def copies(pairs, sems):
    started = []
    for at, (source, target) in enumerate(pairs):
        copy = pltpu.make_async_copy(source, target, sems.at[at])
        copy.start()
        started.append(copy)
    return started


def pick(core, first, second, target, sem):
    @pl.when(core == 0)
    def _():
        pltpu.make_async_copy(first, target, sem).start()

    @pl.when(core != 0)
    def _():
        pltpu.make_async_copy(second, target, sem).start()

    return pltpu.make_async_copy(first, target, sem)


SMEM = pl.BlockSpec(memory_space=pltpu.SMEM)
ANY = pl.BlockSpec(memory_space=pl.ANY)
INNER = pl.BlockSpec(memory_space=pltpu.VMEM)


def cheap():
    return pl.CostEstimate(flops=1 << 20, bytes_accessed=1 << 20, transcendentals=0)


WIDE = 2 * W
STEPS = D // WIDE
GROUPS = Y * XL


def inverse_rows(x_buf, which, inv_buf):
    rows = 64
    for at in range(ROWS // rows):
        part = slice(at * rows, (at + 1) * rows)
        squares = jnp.zeros((rows, 128), F32)
        for j in range(D // 128):
            piece = x_buf[which, part, j * 128 : (j + 1) * 128].astype(F32)
            squares = squares + piece * piece
        mean = jnp.sum(squares, axis=1, keepdims=True) * (1.0 / D)
        inv_buf[which, part, :] = jnp.broadcast_to(lax.rsqrt(mean + EPS), (rows, 128))


def grads_kernel(place_ref, own_ref, other_ref, gain_ref, keys_own_ref, values_own_ref,
                 keys_other_ref, values_other_ref, out_ref, inv_ref,
                 x_buf, d_buf, inv_buf, gain_buf, out_buf, sems, small_sems, out_sems):
    core_at = place_ref[0]
    large = []
    for which, ref in enumerate((own_ref, other_ref)):
        rows = [pl.ds(i * (ROWS // 8), ROWS // 8) for i in range(8)]
        large.append(
            copies([(ref.at[part], x_buf.at[which, part]) for part in rows], sems.at[which])
        )
    small = copies([(gain_ref, gain_buf)], small_sems)
    small.append(pick(core_at, keys_own_ref, values_own_ref, d_buf.at[0], small_sems.at[1]))
    small.append(pick(core_at, keys_other_ref, values_other_ref, d_buf.at[1], small_sems.at[2]))
    for which in range(2):
        for copy in large[which]:
            copy.wait()
        inverse_rows(x_buf, which, inv_buf)
    for copy in small:
        copy.wait()
    sent = [pltpu.make_async_copy(inv_buf.at[0], inv_ref, small_sems.at[3])]
    sent[0].start()
    for part in range(STEPS):
        lanes = slice(part * WIDE, (part + 1) * WIDE)
        total = None
        for which in range(2):
            normal = x_buf[which, :, lanes].astype(F32) * inv_buf[which, :, :1]
            hidden = (normal * gain_buf[:, lanes]).astype(BF)
            term = lax.dot_general(
                hidden, d_buf[which], (((0,), (0,)), ((), ())), preferred_element_type=F32
            )
            total = term if total is None else total + term
        total = total.astype(BF)
        for z in range(WIDE // W):
            for group in range(GROUPS):
                for half in range(XH):
                    for core in range(CORE):
                        first = z * W + (group * CORE + core) * BLOCK
                        out_buf[group * XH + half, part * (WIDE // W) + z, core] = total[
                            first : first + BLOCK, half * HALF : (half + 1) * HALF
                        ]
        zs = pl.ds(part * (WIDE // W), WIDE // W)
        for piece in range(4):
            places = pl.ds(piece * GROUPS * XH // 4, GROUPS * XH // 4)
            copy = pltpu.make_async_copy(
                out_buf.at[places, zs], out_ref.at[places, zs], out_sems.at[part, piece]
            )
            copy.start()
            sent.append(copy)
    for copy in sent:
        copy.wait()


def gradient_terms(*inputs):
    shape = (GROUPS * XH, Z, CORE, BLOCK, HALF)
    return pl.pallas_call(
        grads_kernel,
        in_specs=[SMEM] + [ANY] * 7,
        out_specs=[ANY] * 2,
        out_shape=[
            jax.ShapeDtypeStruct(shape, BF),
            jax.ShapeDtypeStruct((ROWS, 128), F32),
        ],
        scratch_shapes=[
            pltpu.VMEM((2, ROWS, D), BF),
            pltpu.VMEM((2, ROWS, C), BF),
            pltpu.VMEM((2, ROWS, 128), F32),
            pltpu.VMEM((1, D), F32),
            pltpu.VMEM(shape, BF),
            pltpu.SemaphoreType.DMA((2, 8)),
            pltpu.SemaphoreType.DMA((4,)),
            pltpu.SemaphoreType.DMA((STEPS, 4)),
        ],
        compiler_params=params(),
        cost_estimate=cheap(),
        name="gradient_terms",
    )(*inputs)


RING = [(r, 0, GROUPS) for r in range(Z) if r != 4]
RING[4:4] = [(4, 0, GROUPS // 2), (4, GROUPS // 2, GROUPS // 2)]


EXTRA = 16


def pack_kernel(place_ref, in_ref, *refs):
    w_refs = refs[: len(RING)]
    out_ref, prod_ref, w_buf, in_buf, sems, in_sems = refs[len(RING) :]
    group, half = place_ref[2], place_ref[3]
    terms = copies([(in_ref.at[:, z], in_buf.at[:, z]) for z in range(Z)], in_sems)
    waits = []
    for (distance, first, groups), ref in zip(RING, w_refs):
        z = lax.rem(place_ref[1] + Z - distance, Z)
        inside = lax.rem(group, groups)
        copy = pltpu.make_async_copy(
            ref.at[inside, :, half], w_buf.at[pl.ds(z * CORE, CORE)], sems.at[distance]
        )
        if groups == GROUPS:
            copy.start()
        else:
            pl.when(lax.div(group, groups) == first // groups)(copy.start)
        if first == 0:
            waits.append(copy)
    for z in range(Z):
        terms[z].wait()
        for core in range(CORE):
            at = z * CORE + core
            total = in_buf[0, z, core].astype(F32)
            for source in range(1, GROUPS * XH):
                total = total + in_buf[source, z, core].astype(F32)
            out_ref[at, :BLOCK] = total.astype(BF)
            prod_ref[at * BLOCK : (at + 1) * BLOCK] = total
    for copy in waits:
        copy.wait()
    for at in range(Z * CORE):
        rows = slice(at * BLOCK, (at + 1) * BLOCK)
        prod_ref[rows] = prod_ref[rows] * w_buf[at].astype(F32)
    gains = lax.dot_general(
        jnp.ones((8, HALF), F32),
        prod_ref[...],
        (((1,), (1,)), ((), ())),
        precision=lax.Precision.HIGHEST,
        preferred_element_type=F32,
    )[:1]
    upper = gains.astype(BF).astype(F32)
    lower = gains - upper
    row = lax.broadcasted_iota(jnp.int32, (EXTRA, HALF), 0)
    extra = jnp.zeros((EXTRA, HALF), F32)
    for at, line in enumerate(
        (upper[:, :HALF], upper[:, HALF:], lower[:, :HALF], lower[:, HALF:])
    ):
        extra = jnp.where(row == at, jnp.broadcast_to(line, (EXTRA, HALF)), extra)
    extra = extra.astype(BF)
    for at in range(Z * CORE):
        out_ref[at, BLOCK:] = extra


def pack(place, terms, blocks):
    return pl.pallas_call(
        pack_kernel,
        in_specs=[SMEM] + [ANY] * (1 + len(RING)),
        out_specs=INNER,
        out_shape=jax.ShapeDtypeStruct((Z * CORE, BLOCK + EXTRA, HALF), BF),
        scratch_shapes=[
            pltpu.VMEM((Z * CORE * BLOCK, HALF), F32),
            pltpu.VMEM((Z * CORE, BLOCK, HALF), BF),
            pltpu.VMEM(terms.shape, BF),
            pltpu.SemaphoreType.DMA((Z,)),
            pltpu.SemaphoreType.DMA((Z,)),
        ],
        compiler_params=params(),
        cost_estimate=cheap(),
        name="pack",
    )(place, terms, *blocks)


def unpack_kernel(scale, in_ref, key_ref, value_ref, gains_ref):
    for which, ref in enumerate((key_ref, value_ref)):
        total = in_ref[which, :BLOCK].astype(F32)
        for z in range(1, Z):
            total = total + in_ref[z * 2 + which, :BLOCK].astype(F32)
        ref[...] = total * scale
    extra = in_ref[0, BLOCK:].astype(F32)
    for at in range(1, Z * CORE):
        extra = extra + in_ref[at, BLOCK:].astype(F32)
    for line in range(2):
        gains = extra[line : line + 1] + extra[line + 2 : line + 3]
        for piece in range(2):
            lanes = gains[:, piece * 128 : (piece + 1) * 128]
            for at in range(Y * XL * XH):
                gains_ref[at, line * 2 + piece : line * 2 + piece + 1] = lanes


def unpack(scale, received):
    def kernel(*refs):
        unpack_kernel(scale, *refs)

    return pl.pallas_call(
        kernel,
        in_specs=[INNER],
        out_specs=[INNER] * 3,
        out_shape=[
            jax.ShapeDtypeStruct((BLOCK, HALF), F32),
            jax.ShapeDtypeStruct((BLOCK, HALF), F32),
            jax.ShapeDtypeStruct((Y * XL * XH, 4, 128), F32),
        ],
        compiler_params=params(SMALL),
        cost_estimate=cheap(),
        name="unpack",
    )(received)


def weight_rows(buf, part):
    rows = WIDE // BLOCK
    ref = buf.at[pl.ds(part * rows, rows)]
    return jnp.concatenate([ref[:, half].reshape(WIDE, HALF) for half in range(XH)], axis=1)


def rows_kernel(place_ref, x_ref, gain_ref, inv_ref, keys_ref, values_ref, *rest):
    mine, theirs = rest[: len(RING)], rest[len(RING) : 2 * len(RING)]
    (out_keys_ref, out_values_ref, dx_ref, x_buf, w_buf, d_buf, inv_buf, gain_buf, out_buf, dx_buf,
     sems, small_sems, out_sems, dx_sems) = rest[2 * len(RING) :]
    core = place_ref[0]
    rows = W // BLOCK

    def columns(at):
        z = lax.rem(place_ref[1] + Z - at, Z)
        return pl.ds(pl.multiple_of(z * W, W), W)

    def fetch(part):
        pairs = []
        for at in range(part * WIDE // W, (part + 1) * WIDE // W):
            lanes = pl.ds(at * W, W)
            pairs.append((x_ref.at[:, columns(at)], x_buf.at[:, lanes]))
            pairs.append((gain_ref.at[:, columns(at)], gain_buf.at[:, lanes]))
            for which, refs in enumerate((mine, theirs)):
                for (distance, first, groups), ref in zip(RING, refs):
                    if distance == at:
                        block = pl.ds(at * rows + first * CORE, groups * CORE)
                        pairs.append((ref, w_buf.at[which, block]))
        return copies(pairs, sems.at[part])

    large = [fetch(0)]
    small = copies([(inv_ref, inv_buf)], small_sems)
    small.append(pick(core, keys_ref, values_ref, d_buf.at[0], small_sems.at[1]))
    small.append(pick(core, values_ref, keys_ref, d_buf.at[1], small_sems.at[2]))
    large.append(fetch(1))
    small[0].wait()
    totals = [None, None]
    for part in range(STEPS):
        for copy in large[part]:
            copy.wait()
        if part + 2 < STEPS:
            large.append(fetch(part + 2))
        lanes = slice(part * WIDE, (part + 1) * WIDE)
        normal = x_buf[:, lanes].astype(F32) * inv_buf[:, :1]
        hidden = (normal * gain_buf[:, lanes]).astype(BF)
        for which in range(2):
            weights = weight_rows(w_buf.at[which], part)
            term = jnp.dot(hidden, weights, preferred_element_type=F32)
            totals[which] = term if totals[which] is None else totals[which] + term
    for copy in small[1:]:
        copy.wait()
    sent = []
    along = None
    for which in range(2):
        out_buf[which] = totals[which].astype(BF)
        refs = (out_keys_ref, out_values_ref) if which == 0 else (out_values_ref, out_keys_ref)

        @pl.when(core == 0)
        def _():
            pltpu.make_async_copy(out_buf.at[which], refs[0], out_sems.at[which]).start()

        @pl.when(core != 0)
        def _():
            pltpu.make_async_copy(out_buf.at[which], refs[1], out_sems.at[which]).start()

        sent.append(pltpu.make_async_copy(out_buf.at[which], refs[0], out_sems.at[which]))
        term = jnp.sum(totals[which] * d_buf[which].astype(F32), axis=1, keepdims=True)
        along = term if along is None else along + term
    along = along * (1.0 / D)
    inverse = inv_buf[:, :1]
    for part in range(STEPS):
        lanes = slice(part * WIDE, (part + 1) * WIDE)
        d_hidden = None
        for which in range(2):
            term = lax.dot_general(
                d_buf[which],
                weight_rows(w_buf.at[which], part),
                (((1,), (1,)), ((), ())),
                preferred_element_type=F32,
            )
            d_hidden = term if d_hidden is None else d_hidden + term
        normal = x_buf[:, lanes].astype(F32) * inverse
        dx_buf[:, lanes] = (inverse * (d_hidden * gain_buf[:, lanes] - normal * along)).astype(BF)
        for piece in range(WIDE // W):
            at = part * (WIDE // W) + piece
            copy = pltpu.make_async_copy(
                dx_buf.at[:, pl.ds(at * W, W)], dx_ref.at[:, columns(at)], dx_sems.at[part, piece]
            )
            copy.start()
            sent.append(copy)
    for copy in sent:
        copy.wait()


def rows_pass(*inputs):
    return pl.pallas_call(
        rows_kernel,
        in_specs=[SMEM] + [ANY] * (5 + 2 * len(RING)),
        out_specs=[ANY] * 3,
        out_shape=[
            jax.ShapeDtypeStruct((ROWS, C), BF),
            jax.ShapeDtypeStruct((ROWS, C), BF),
            jax.ShapeDtypeStruct((ROWS, D), BF),
        ],
        scratch_shapes=[
            pltpu.VMEM((ROWS, D), BF),
            pltpu.VMEM((2, D // BLOCK, XH, BLOCK, HALF), BF),
            pltpu.VMEM((2, ROWS, C), BF),
            pltpu.VMEM((ROWS, 128), F32),
            pltpu.VMEM((1, D), F32),
            pltpu.VMEM((2, ROWS, C), BF),
            pltpu.VMEM((ROWS, D), BF),
            pltpu.SemaphoreType.DMA((STEPS, 10)),
            pltpu.SemaphoreType.DMA((3,)),
            pltpu.SemaphoreType.DMA((2,)),
            pltpu.SemaphoreType.DMA((STEPS, WIDE // W)),
        ],
        compiler_params=params(),
        cost_estimate=pl.CostEstimate(
            flops=8 * ROWS * D * C, bytes_accessed=18 << 20, transcendentals=0
        ),
        name="rows_pass",
    )(*inputs)


def finish_kernel(scale, in_ref, gain_ref, out_ref):
    sums_of = [in_ref[at * XH] + in_ref[at * XH + 1] for at in range(Y * XL)]
    for z in range(Z):
        line, lanes = z // 2, slice(z % 2 * 64, z % 2 * 64 + 64)
        for at in range(0, Y * XL, 2):
            first, second = (sums_of[at + i][line : line + 1, lanes] for i in range(2))
            tile = jnp.concatenate([first, second], axis=1) * scale
            span = slice(z * W + at * 64, z * W + at * 64 + 128)
            out_ref[:, span] = tile / gain_ref[:, span]


def finish(scale, gains, gain):
    def kernel(*refs):
        finish_kernel(scale, *refs)

    return pl.pallas_call(
        kernel,
        in_specs=[INNER] * 2,
        out_specs=INNER,
        out_shape=jax.ShapeDtypeStruct((1, D), F32),
        compiler_params=params(SMALL),
        cost_estimate=cheap(),
        name="finish",
    )(gains, gain)


def swap(a):
    return lax.ppermute(a, "core", [(0, 1), (1, 0)])


def along_z(a, step):
    return lax.ppermute(a, "z", [(i, (i + step) % Z) for i in range(Z)])


def around(own):
    up, down = [own], [own]
    for _ in range(3):
        up.append(along_z(up[-1], 1))
        down.append(along_z(down[-1], -1))
    last = [along_z(up[3][: GROUPS // 2], 1), along_z(down[3][GROUPS // 2 :], -1)]
    return up + last + down[:0:-1]


def shards(tokens, gain, w_key, w_value, d_keys, d_values):
    scale = 1.0 / math.sqrt(ROWS * Z * Y * XL * CORE * XH)
    y_at, low, high = lax.axis_index("y"), lax.axis_index("xl"), lax.axis_index("xh")
    core, z_at = lax.axis_index("core"), lax.axis_index("z")
    place = jnp.stack([core, z_at, y_at * XL + low, high]).astype(jnp.int32)
    row_gain = gain.reshape(1, D)

    pair = jnp.stack([w_key, w_value])
    sent = jnp.broadcast_to(pair[None, :, None], (Y * XL, CORE, XH, BLOCK, HALF))
    plane = lax.all_to_all(
        sent.reshape(Y * XL * CORE * XH, BLOCK, HALF), ("y", "xl", "core", "xh"), 0, 0, tiled=True
    )

    inputs = (place, tokens, swap(tokens), row_gain, d_keys, d_values, swap(d_keys), swap(d_values))
    terms, inv = gradient_terms(*inputs)
    plane = after(plane, inv).reshape(GROUPS, CORE, XH, BLOCK, HALF)
    mine = around(plane)
    theirs = [swap(block) for block in mine]

    sent = pack(place, lax.all_to_all(terms, PLANE, 0, 0, tiled=True), mine)
    received = lax.all_to_all(sent, ("z", "core"), 0, 0, tiled=True)

    flat = [block.reshape(-1, XH, BLOCK, HALF) for block in mine + theirs]
    keys, values, d_tokens = rows_pass(place, tokens, row_gain, inv, d_keys, d_values, *flat)
    grad_key, grad_value, gains = unpack(scale, after(received, d_tokens))
    gains = lax.all_to_all(gains, PLANE, 0, 0, tiled=True)
    grad_gain = finish(scale, gains, row_gain).reshape(D)
    return (keys, values, d_tokens, grad_key, grad_value, grad_gain)


def solution(mesh):
    fine = Mesh(mesh.devices.reshape(Z, Y, XL, CORE, XH), AXES)
    loop = ("z", "y", "xl", "core")
    return jax.shard_map(
        shards,
        mesh=fine,
        in_specs=(
            P(AXES, None),
            P(),
            P(loop, "xh"),
            P(loop, "xh"),
            P(AXES, None),
            P(AXES, None),
        ),
        out_specs=(
            P(AXES, None),
            P(AXES, None),
            P(AXES, None),
            P(loop, "xh"),
            P(loop, "xh"),
            P(),
        ),
        check_vma=False,
    )
```

```python
import math

import jax
import jax.numpy as jnp
from jax import lax
from jax.experimental import pallas as pl
from jax.experimental.pallas import tpu as pltpu
from jax.sharding import Mesh
from jax.sharding import PartitionSpec as P

Z, Y, XL, CORE, XH = 8, 4, 2, 2, 2
AXES = ("z", "y", "xl", "core", "xh")
PLANE = ("y", "xl", "xh")
ROWS = 512
D = 4096
C = 512
W = D // Z
HALF = C // XH
BLOCK = 32
EPS = 1e-05
BF = jnp.bfloat16
F32 = jnp.float32
VMEM = 60 * 1024 * 1024
SMALL = 8 * 1024 * 1024


def params(limit=VMEM):
    return pltpu.CompilerParams(vmem_limit_bytes=limit)


def tie_kernel(a_ref, other_ref, out_ref):
    del a_ref, other_ref, out_ref


def after(a, other):
    return pl.pallas_call(
        tie_kernel,
        in_specs=[pl.BlockSpec(memory_space=pl.ANY)] * 2,
        out_specs=pl.BlockSpec(memory_space=pl.ANY),
        out_shape=jax.ShapeDtypeStruct(a.shape, a.dtype),
        input_output_aliases={0: 0},
        cost_estimate=pl.CostEstimate(flops=0, bytes_accessed=0, transcendentals=0),
        name="after",
    )(a, other)


def copies(pairs, sems):
    started = []
    for at, (source, target) in enumerate(pairs):
        copy = pltpu.make_async_copy(source, target, sems.at[at])
        copy.start()
        started.append(copy)
    return started


def pick(core, first, second, target, sem):
    @pl.when(core == 0)
    def _():
        pltpu.make_async_copy(first, target, sem).start()

    @pl.when(core != 0)
    def _():
        pltpu.make_async_copy(second, target, sem).start()

    return pltpu.make_async_copy(first, target, sem)


ANY = pl.BlockSpec(memory_space=pl.ANY)
INNER = pl.BlockSpec(memory_space=pltpu.VMEM)


def cheap():
    return pl.CostEstimate(flops=1 << 20, bytes_accessed=1 << 20, transcendentals=0)


WIDE = 2 * W
STEPS = D // WIDE
GROUPS = Y * XL


def inverse_rows(x_buf, which, inv_buf):
    rows = 64
    for at in range(ROWS // rows):
        part = slice(at * rows, (at + 1) * rows)
        squares = jnp.zeros((rows, 128), F32)
        for j in range(D // 128):
            piece = x_buf[which, part, j * 128 : (j + 1) * 128].astype(F32)
            squares = squares + piece * piece
        mean = jnp.sum(squares, axis=1, keepdims=True) * (1.0 / D)
        inv_buf[which, part, :] = jnp.broadcast_to(lax.rsqrt(mean + EPS), (rows, 128))


def grads_kernel(own_ref, other_ref, gain_ref, keys_own_ref, values_own_ref,
                 keys_other_ref, values_other_ref, out_ref, inv_ref,
                 x_buf, d_buf, inv_buf, gain_buf, out_buf, sems, small_sems, out_sems):
    core_at = lax.axis_index("core")
    large = []
    for which, ref in enumerate((own_ref, other_ref)):
        rows = [pl.ds(i * (ROWS // 8), ROWS // 8) for i in range(8)]
        large.append(
            copies([(ref.at[part], x_buf.at[which, part]) for part in rows], sems.at[which])
        )
    small = copies([(gain_ref, gain_buf)], small_sems)
    small.append(pick(core_at, keys_own_ref, values_own_ref, d_buf.at[0], small_sems.at[1]))
    small.append(pick(core_at, keys_other_ref, values_other_ref, d_buf.at[1], small_sems.at[2]))
    for which in range(2):
        for copy in large[which]:
            copy.wait()
        inverse_rows(x_buf, which, inv_buf)
    for copy in small:
        copy.wait()
    sent = [pltpu.make_async_copy(inv_buf.at[0], inv_ref, small_sems.at[3])]
    sent[0].start()
    for part in range(STEPS):
        lanes = slice(part * WIDE, (part + 1) * WIDE)
        total = None
        for which in range(2):
            normal = x_buf[which, :, lanes].astype(F32) * inv_buf[which, :, :1]
            hidden = (normal * gain_buf[:, lanes]).astype(BF)
            term = lax.dot_general(
                hidden, d_buf[which], (((0,), (0,)), ((), ())), preferred_element_type=F32
            )
            total = term if total is None else total + term
        total = total.astype(BF)
        for z in range(WIDE // W):
            for group in range(GROUPS):
                for half in range(XH):
                    for core in range(CORE):
                        first = z * W + (group * CORE + core) * BLOCK
                        out_buf[group * XH + half, part * (WIDE // W) + z, core] = total[
                            first : first + BLOCK, half * HALF : (half + 1) * HALF
                        ]
        zs = pl.ds(part * (WIDE // W), WIDE // W)
        for piece in range(4):
            places = pl.ds(piece * GROUPS * XH // 4, GROUPS * XH // 4)
            copy = pltpu.make_async_copy(
                out_buf.at[places, zs], out_ref.at[places, zs], out_sems.at[part, piece]
            )
            copy.start()
            sent.append(copy)
    for copy in sent:
        copy.wait()


def gradient_terms(*inputs):
    shape = (GROUPS * XH, Z, CORE, BLOCK, HALF)
    return pl.pallas_call(
        grads_kernel,
        in_specs=[ANY] * 7,
        out_specs=[ANY] * 2,
        out_shape=[
            jax.ShapeDtypeStruct(shape, BF),
            jax.ShapeDtypeStruct((ROWS, 128), F32),
        ],
        scratch_shapes=[
            pltpu.VMEM((2, ROWS, D), BF),
            pltpu.VMEM((2, ROWS, C), BF),
            pltpu.VMEM((2, ROWS, 128), F32),
            pltpu.VMEM((1, D), F32),
            pltpu.VMEM(shape, BF),
            pltpu.SemaphoreType.DMA((2, 8)),
            pltpu.SemaphoreType.DMA((4,)),
            pltpu.SemaphoreType.DMA((STEPS, 4)),
        ],
        compiler_params=params(),
        cost_estimate=cheap(),
        name="gradient_terms",
    )(*inputs)


RING = [(r, 0, GROUPS) for r in range(Z) if r != 4]
RING[4:4] = [(4, 0, GROUPS // 2), (4, GROUPS // 2, GROUPS // 2)]


EXTRA = 16


def pack_kernel(in_ref, *refs):
    w_refs = refs[: len(RING)]
    out_ref, prod_ref, w_buf, in_buf, sems, in_sems = refs[len(RING) :]
    group = lax.axis_index("y") * XL + lax.axis_index("xl")
    half, z_at = lax.axis_index("xh"), lax.axis_index("z")
    terms = copies([(in_ref.at[:, z], in_buf.at[:, z]) for z in range(Z)], in_sems)
    waits = []
    for (distance, first, groups), ref in zip(RING, w_refs):
        z = lax.rem(z_at + Z - distance, Z)
        inside = lax.rem(group, groups)
        copy = pltpu.make_async_copy(
            ref.at[inside, :, half], w_buf.at[pl.ds(z * CORE, CORE)], sems.at[distance]
        )
        if groups == GROUPS:
            copy.start()
        else:
            pl.when(lax.div(group, groups) == first // groups)(copy.start)
        if first == 0:
            waits.append(copy)
    for z in range(Z):
        terms[z].wait()
        for core in range(CORE):
            at = z * CORE + core
            total = in_buf[0, z, core].astype(F32)
            for source in range(1, GROUPS * XH):
                total = total + in_buf[source, z, core].astype(F32)
            out_ref[at, :BLOCK] = total.astype(BF)
            prod_ref[at * BLOCK : (at + 1) * BLOCK] = total
    for copy in waits:
        copy.wait()
    for at in range(Z * CORE):
        rows = slice(at * BLOCK, (at + 1) * BLOCK)
        prod_ref[rows] = prod_ref[rows] * w_buf[at].astype(F32)
    gains = lax.dot_general(
        jnp.ones((8, HALF), F32),
        prod_ref[...],
        (((1,), (1,)), ((), ())),
        precision=lax.Precision.HIGHEST,
        preferred_element_type=F32,
    )[:1]
    upper = gains.astype(BF).astype(F32)
    lower = gains - upper
    row = lax.broadcasted_iota(jnp.int32, (EXTRA, HALF), 0)
    extra = jnp.zeros((EXTRA, HALF), F32)
    for at, line in enumerate(
        (upper[:, :HALF], upper[:, HALF:], lower[:, :HALF], lower[:, HALF:])
    ):
        extra = jnp.where(row == at, jnp.broadcast_to(line, (EXTRA, HALF)), extra)
    extra = extra.astype(BF)
    for at in range(Z * CORE):
        out_ref[at, BLOCK:] = extra


def pack(terms, blocks):
    return pl.pallas_call(
        pack_kernel,
        in_specs=[ANY] * (1 + len(RING)),
        out_specs=INNER,
        out_shape=jax.ShapeDtypeStruct((Z * CORE, BLOCK + EXTRA, HALF), BF),
        scratch_shapes=[
            pltpu.VMEM((Z * CORE * BLOCK, HALF), F32),
            pltpu.VMEM((Z * CORE, BLOCK, HALF), BF),
            pltpu.VMEM(terms.shape, BF),
            pltpu.SemaphoreType.DMA((Z,)),
            pltpu.SemaphoreType.DMA((Z,)),
        ],
        compiler_params=params(),
        cost_estimate=cheap(),
        name="pack",
    )(terms, *blocks)


def unpack_kernel(scale, in_ref, rows_ref, key_ref, value_ref, gains_ref):
    for which, ref in enumerate((key_ref, value_ref)):
        total = in_ref[which, :BLOCK].astype(F32)
        for z in range(1, Z):
            total = total + in_ref[z * 2 + which, :BLOCK].astype(F32)
        ref[...] = total * scale
    extra = in_ref[0, BLOCK:].astype(F32)
    for at in range(1, Z * CORE):
        extra = extra + in_ref[at, BLOCK:].astype(F32)
    for line in range(2):
        gains = extra[line : line + 1] + extra[line + 2 : line + 3]
        for piece in range(2):
            lanes = gains[:, piece * 128 : (piece + 1) * 128]
            for at in range(Y * XL * XH):
                gains_ref[at, line * 2 + piece : line * 2 + piece + 1] = lanes


def unpack(scale, received, rows):
    def kernel(*refs):
        unpack_kernel(scale, *refs)

    return pl.pallas_call(
        kernel,
        in_specs=[INNER, ANY],
        out_specs=[INNER] * 3,
        out_shape=[
            jax.ShapeDtypeStruct((BLOCK, HALF), F32),
            jax.ShapeDtypeStruct((BLOCK, HALF), F32),
            jax.ShapeDtypeStruct((Y * XL * XH, 4, 128), F32),
        ],
        compiler_params=params(),
        cost_estimate=cheap(),
        name="unpack",
    )(received, rows)


def weight_rows(buf, part):
    rows = WIDE // BLOCK
    ref = buf.at[pl.ds(part * rows, rows)]
    return jnp.concatenate([ref[:, half].reshape(WIDE, HALF) for half in range(XH)], axis=1)


def rows_kernel(x_ref, gain_ref, inv_ref, keys_ref, values_ref, *rest):
    mine, theirs = rest[: len(RING)], rest[len(RING) : 2 * len(RING)]
    (out_keys_ref, out_values_ref, dx_ref, x_buf, w_buf, d_buf, inv_buf, gain_buf, out_buf, dx_buf,
     sems, small_sems, out_sems, dx_sems) = rest[2 * len(RING) :]
    core = lax.axis_index("core")
    rows = W // BLOCK

    def columns(at):
        z = lax.rem(lax.axis_index("z") + Z - at, Z)
        return pl.ds(pl.multiple_of(z * W, W), W)

    def fetch(part):
        pairs = []
        for at in range(part * WIDE // W, (part + 1) * WIDE // W):
            lanes = pl.ds(at * W, W)
            pairs.append((x_ref.at[:, columns(at)], x_buf.at[:, lanes]))
            pairs.append((gain_ref.at[:, columns(at)], gain_buf.at[:, lanes]))
            for which, refs in enumerate((mine, theirs)):
                for (distance, first, groups), ref in zip(RING, refs):
                    if distance == at:
                        block = pl.ds(at * rows + first * CORE, groups * CORE)
                        pairs.append((ref, w_buf.at[which, block]))
        return copies(pairs, sems.at[part])

    large = [fetch(0)]
    small = copies([(inv_ref, inv_buf)], small_sems)
    small.append(pick(core, keys_ref, values_ref, d_buf.at[0], small_sems.at[1]))
    small.append(pick(core, values_ref, keys_ref, d_buf.at[1], small_sems.at[2]))
    large.append(fetch(1))
    small[0].wait()
    totals = [None, None]
    for part in range(STEPS):
        for copy in large[part]:
            copy.wait()
        if part + 2 < STEPS:
            large.append(fetch(part + 2))
        lanes = slice(part * WIDE, (part + 1) * WIDE)
        normal = x_buf[:, lanes].astype(F32) * inv_buf[:, :1]
        hidden = (normal * gain_buf[:, lanes]).astype(BF)
        for which in range(2):
            weights = weight_rows(w_buf.at[which], part)
            term = jnp.dot(hidden, weights, preferred_element_type=F32)
            totals[which] = term if totals[which] is None else totals[which] + term
    for copy in small[1:]:
        copy.wait()
    sent = []
    along = None
    for which in range(2):
        out_buf[which] = totals[which].astype(BF)
        refs = (out_keys_ref, out_values_ref) if which == 0 else (out_values_ref, out_keys_ref)

        @pl.when(core == 0)
        def _():
            pltpu.make_async_copy(out_buf.at[which], refs[0], out_sems.at[which]).start()

        @pl.when(core != 0)
        def _():
            pltpu.make_async_copy(out_buf.at[which], refs[1], out_sems.at[which]).start()

        sent.append(pltpu.make_async_copy(out_buf.at[which], refs[0], out_sems.at[which]))
        term = jnp.sum(totals[which] * d_buf[which].astype(F32), axis=1, keepdims=True)
        along = term if along is None else along + term
    along = along * (1.0 / D)
    inverse = inv_buf[:, :1]
    for part in range(STEPS):
        lanes = slice(part * WIDE, (part + 1) * WIDE)
        d_hidden = None
        for which in range(2):
            term = lax.dot_general(
                d_buf[which],
                weight_rows(w_buf.at[which], part),
                (((1,), (1,)), ((), ())),
                preferred_element_type=F32,
            )
            d_hidden = term if d_hidden is None else d_hidden + term
        normal = x_buf[:, lanes].astype(F32) * inverse
        dx_buf[:, lanes] = (inverse * (d_hidden * gain_buf[:, lanes] - normal * along)).astype(BF)
        for piece in range(WIDE // W):
            at = part * (WIDE // W) + piece
            copy = pltpu.make_async_copy(
                dx_buf.at[:, pl.ds(at * W, W)], dx_ref.at[:, columns(at)], dx_sems.at[part, piece]
            )
            copy.start()
            sent.append(copy)
    for copy in sent:
        copy.wait()


def rows_pass(*inputs):
    return pl.pallas_call(
        rows_kernel,
        in_specs=[ANY] * (5 + 2 * len(RING)),
        out_specs=[ANY] * 3,
        out_shape=[
            jax.ShapeDtypeStruct((ROWS, C), BF),
            jax.ShapeDtypeStruct((ROWS, C), BF),
            jax.ShapeDtypeStruct((ROWS, D), BF),
        ],
        scratch_shapes=[
            pltpu.VMEM((ROWS, D), BF),
            pltpu.VMEM((2, D // BLOCK, XH, BLOCK, HALF), BF),
            pltpu.VMEM((2, ROWS, C), BF),
            pltpu.VMEM((ROWS, 128), F32),
            pltpu.VMEM((1, D), F32),
            pltpu.VMEM((2, ROWS, C), BF),
            pltpu.VMEM((ROWS, D), BF),
            pltpu.SemaphoreType.DMA((STEPS, 10)),
            pltpu.SemaphoreType.DMA((3,)),
            pltpu.SemaphoreType.DMA((2,)),
            pltpu.SemaphoreType.DMA((STEPS, WIDE // W)),
        ],
        compiler_params=params(),
        cost_estimate=pl.CostEstimate(
            flops=8 * ROWS * D * C, bytes_accessed=18 << 20, transcendentals=0
        ),
        name="rows_pass",
    )(*inputs)


def finish_kernel(scale, in_ref, gain_ref, out_ref):
    sums_of = [in_ref[at * XH] + in_ref[at * XH + 1] for at in range(Y * XL)]
    for z in range(Z):
        line, lanes = z // 2, slice(z % 2 * 64, z % 2 * 64 + 64)
        for at in range(0, Y * XL, 2):
            first, second = (sums_of[at + i][line : line + 1, lanes] for i in range(2))
            tile = jnp.concatenate([first, second], axis=1) * scale
            span = slice(z * W + at * 64, z * W + at * 64 + 128)
            out_ref[:, span] = tile / gain_ref[:, span]


def finish(scale, gains, gain):
    def kernel(*refs):
        finish_kernel(scale, *refs)

    return pl.pallas_call(
        kernel,
        in_specs=[INNER] * 2,
        out_specs=INNER,
        out_shape=jax.ShapeDtypeStruct((1, D), F32),
        compiler_params=params(SMALL),
        cost_estimate=cheap(),
        name="finish",
    )(gains, gain)


def swap(a):
    return lax.ppermute(a, "core", [(0, 1), (1, 0)])


def along_z(a, step):
    return lax.ppermute(a, "z", [(i, (i + step) % Z) for i in range(Z)])


def around(own):
    up, down = [own], [own]
    for _ in range(3):
        up.append(along_z(up[-1], 1))
        down.append(along_z(down[-1], -1))
    last = [along_z(up[3][: GROUPS // 2], 1), along_z(down[3][GROUPS // 2 :], -1)]
    return up + last + down[:0:-1]


def shards(tokens, gain, w_key, w_value, d_keys, d_values):
    scale = 1.0 / math.sqrt(ROWS * Z * Y * XL * CORE * XH)
    row_gain = gain.reshape(1, D)

    which = lax.broadcasted_iota(jnp.int32, (Y * XL, CORE, XH, BLOCK, HALF), 1)
    sent = jnp.where(which == 0, w_key[None, None, None], w_value[None, None, None])
    plane = lax.all_to_all(
        sent.reshape(Y * XL * CORE * XH, BLOCK, HALF), ("y", "xl", "core", "xh"), 0, 0, tiled=True
    )

    inputs = (tokens, swap(tokens), row_gain, d_keys, d_values, swap(d_keys), swap(d_values))
    terms, inv = gradient_terms(*inputs)
    plane = plane.reshape(GROUPS, CORE, XH, BLOCK, HALF)
    mine = around(plane)
    theirs = [swap(block) for block in mine]

    sent = pack(lax.all_to_all(terms, PLANE, 0, 0, tiled=True), mine)
    received = lax.all_to_all(sent, ("z", "core"), 0, 0, tiled=True)

    flat = [block.reshape(-1, XH, BLOCK, HALF) for block in mine + theirs]
    keys, values, d_tokens = rows_pass(tokens, row_gain, inv, d_keys, d_values, *flat)
    grad_key, grad_value, gains = unpack(scale, received, keys)
    gains = lax.all_to_all(gains, PLANE, 0, 0, tiled=True)
    grad_gain = finish(scale, gains, row_gain).reshape(D)
    return (keys, values, d_tokens, grad_key, grad_value, grad_gain)


def solution(mesh):
    fine = Mesh(mesh.devices.reshape(Z, Y, XL, CORE, XH), AXES)
    loop = ("z", "y", "xl", "core")
    return jax.shard_map(
        shards,
        mesh=fine,
        in_specs=(
            P(AXES, None),
            P(),
            P(loop, "xh"),
            P(loop, "xh"),
            P(AXES, None),
            P(AXES, None),
        ),
        out_specs=(
            P(AXES, None),
            P(AXES, None),
            P(AXES, None),
            P(loop, "xh"),
            P(loop, "xh"),
            P(),
        ),
        check_vma=False,
    )
```

```python
import math

import jax
import jax.numpy as jnp
from jax import lax
from jax.experimental import pallas as pl
from jax.experimental.pallas import tpu as pltpu
from jax.sharding import Mesh
from jax.sharding import PartitionSpec as P

Z, Y, XL, CORE, XH = 8, 4, 2, 2, 2
AXES = ("z", "y", "xl", "core", "xh")
PLANE = ("y", "xl", "xh")
ROWS = 512
D = 4096
C = 512
W = D // Z
HALF = C // XH
BLOCK = 32
EPS = 1e-05
BF = jnp.bfloat16
F32 = jnp.float32
VMEM = 60 * 1024 * 1024
SMALL = 8 * 1024 * 1024


def params(limit=VMEM):
    return pltpu.CompilerParams(vmem_limit_bytes=limit)


def tie_kernel(a_ref, other_ref, out_ref):
    del a_ref, other_ref, out_ref


def after(a, other):
    return pl.pallas_call(
        tie_kernel,
        in_specs=[pl.BlockSpec(memory_space=pl.ANY)] * 2,
        out_specs=pl.BlockSpec(memory_space=pl.ANY),
        out_shape=jax.ShapeDtypeStruct(a.shape, a.dtype),
        input_output_aliases={0: 0},
        cost_estimate=pl.CostEstimate(flops=0, bytes_accessed=0, transcendentals=0),
        name="after",
    )(a, other)


def copies(pairs, sems):
    started = []
    for at, (source, target) in enumerate(pairs):
        copy = pltpu.make_async_copy(source, target, sems.at[at])
        copy.start()
        started.append(copy)
    return started


def pick(core, first, second, target, sem):
    @pl.when(core == 0)
    def _():
        pltpu.make_async_copy(first, target, sem).start()

    @pl.when(core != 0)
    def _():
        pltpu.make_async_copy(second, target, sem).start()

    return pltpu.make_async_copy(first, target, sem)


ANY = pl.BlockSpec(memory_space=pl.ANY)
INNER = pl.BlockSpec(memory_space=pltpu.VMEM)


def cheap():
    return pl.CostEstimate(flops=1 << 20, bytes_accessed=1 << 20, transcendentals=0)


WIDE = 2 * W
STEPS = D // WIDE
GROUPS = Y * XL


def inverse_rows(x_buf, which, inv_buf):
    rows = 64
    for at in range(ROWS // rows):
        part = slice(at * rows, (at + 1) * rows)
        squares = jnp.zeros((rows, 128), F32)
        for j in range(D // 128):
            piece = x_buf[which, part, j * 128 : (j + 1) * 128].astype(F32)
            squares = squares + piece * piece
        mean = jnp.sum(squares, axis=1, keepdims=True) * (1.0 / D)
        inv_buf[which, part, :] = jnp.broadcast_to(lax.rsqrt(mean + EPS), (rows, 128))


def grads_kernel(own_ref, other_ref, keys_own_ref, values_own_ref,
                 keys_other_ref, values_other_ref, out_ref, inv_ref,
                 x_buf, d_buf, scaled_buf, inv_buf, out_buf, sems, small_sems, out_sems):
    core_at = lax.axis_index("core")
    large = []
    for which, ref in enumerate((own_ref, other_ref)):
        rows = [pl.ds(i * (ROWS // 8), ROWS // 8) for i in range(8)]
        large.append(
            copies([(ref.at[part], x_buf.at[which, part]) for part in rows], sems.at[which])
        )
    small = [
        pick(core_at, keys_own_ref, values_own_ref, d_buf.at[0], small_sems.at[0]),
        pick(core_at, keys_other_ref, values_other_ref, d_buf.at[1], small_sems.at[1]),
    ]
    for which in range(2):
        for copy in large[which]:
            copy.wait()
        inverse_rows(x_buf, which, inv_buf)
        small[which].wait()
        scaled_buf[which] = (d_buf[which].astype(F32) * inv_buf[which, :, :1]).astype(BF)
    sent = [pltpu.make_async_copy(inv_buf.at[0], inv_ref, small_sems.at[2])]
    sent[0].start()
    for part in range(STEPS):
        lanes = slice(part * WIDE, (part + 1) * WIDE)
        total = None
        for which in range(2):
            term = lax.dot_general(
                x_buf[which, :, lanes],
                scaled_buf[which],
                (((0,), (0,)), ((), ())),
                preferred_element_type=F32,
            )
            total = term if total is None else total + term
        total = total.astype(BF)
        for z in range(WIDE // W):
            for group in range(GROUPS):
                for half in range(XH):
                    for core in range(CORE):
                        first = z * W + (group * CORE + core) * BLOCK
                        out_buf[group * XH + half, part * (WIDE // W) + z, core] = total[
                            first : first + BLOCK, half * HALF : (half + 1) * HALF
                        ]
        zs = pl.ds(part * (WIDE // W), WIDE // W)
        for piece in range(4):
            places = pl.ds(piece * GROUPS * XH // 4, GROUPS * XH // 4)
            copy = pltpu.make_async_copy(
                out_buf.at[places, zs], out_ref.at[places, zs], out_sems.at[part, piece]
            )
            copy.start()
            sent.append(copy)
    for copy in sent:
        copy.wait()


def gradient_terms(*inputs):
    shape = (GROUPS * XH, Z, CORE, BLOCK, HALF)
    return pl.pallas_call(
        grads_kernel,
        in_specs=[ANY] * 6,
        out_specs=[ANY] * 2,
        out_shape=[
            jax.ShapeDtypeStruct(shape, BF),
            jax.ShapeDtypeStruct((ROWS, 128), F32),
        ],
        scratch_shapes=[
            pltpu.VMEM((2, ROWS, D), BF),
            pltpu.VMEM((2, ROWS, C), BF),
            pltpu.VMEM((2, ROWS, C), BF),
            pltpu.VMEM((2, ROWS, 128), F32),
            pltpu.VMEM(shape, BF),
            pltpu.SemaphoreType.DMA((2, 8)),
            pltpu.SemaphoreType.DMA((3,)),
            pltpu.SemaphoreType.DMA((STEPS, 4)),
        ],
        compiler_params=params(),
        cost_estimate=cheap(),
        name="gradient_terms",
    )(*inputs)


RING = [(r, 0, GROUPS) for r in range(Z) if r != 4]
RING[4:4] = [(4, 0, GROUPS // 2), (4, GROUPS // 2, GROUPS // 2)]


EXTRA = 16


def pack_kernel(in_ref, *refs):
    w_refs = refs[: len(RING)]
    out_ref, prod_ref, w_buf, in_buf, sems, in_sems = refs[len(RING) :]
    group = lax.axis_index("y") * XL + lax.axis_index("xl")
    half, z_at = lax.axis_index("xh"), lax.axis_index("z")
    terms = copies([(in_ref.at[:, z], in_buf.at[:, z]) for z in range(Z)], in_sems)
    waits = []
    for (distance, first, groups), ref in zip(RING, w_refs):
        z = lax.rem(z_at + Z - distance, Z)
        inside = lax.rem(group, groups)
        copy = pltpu.make_async_copy(
            ref.at[inside, :, half], w_buf.at[pl.ds(z * CORE, CORE)], sems.at[distance]
        )
        if groups == GROUPS:
            copy.start()
        else:
            pl.when(lax.div(group, groups) == first // groups)(copy.start)
        if first == 0:
            waits.append(copy)
    for z in range(Z):
        terms[z].wait()
        for core in range(CORE):
            at = z * CORE + core
            total = in_buf[0, z, core].astype(F32)
            for source in range(1, GROUPS * XH):
                total = total + in_buf[source, z, core].astype(F32)
            out_ref[at, :BLOCK] = total.astype(BF)
            prod_ref[at * BLOCK : (at + 1) * BLOCK] = total
    for copy in waits:
        copy.wait()
    for at in range(Z * CORE):
        rows = slice(at * BLOCK, (at + 1) * BLOCK)
        prod_ref[rows] = prod_ref[rows] * w_buf[at].astype(F32)
    gains = lax.dot_general(
        jnp.ones((8, HALF), F32),
        prod_ref[...],
        (((1,), (1,)), ((), ())),
        precision=lax.Precision.HIGHEST,
        preferred_element_type=F32,
    )[:1]
    upper = gains.astype(BF).astype(F32)
    lower = gains - upper
    row = lax.broadcasted_iota(jnp.int32, (EXTRA, HALF), 0)
    extra = jnp.zeros((EXTRA, HALF), F32)
    for at, line in enumerate(
        (upper[:, :HALF], upper[:, HALF:], lower[:, :HALF], lower[:, HALF:])
    ):
        extra = jnp.where(row == at, jnp.broadcast_to(line, (EXTRA, HALF)), extra)
    extra = extra.astype(BF)
    for at in range(Z * CORE):
        out_ref[at, BLOCK:] = extra


def pack(terms, blocks):
    return pl.pallas_call(
        pack_kernel,
        in_specs=[ANY] * (1 + len(RING)),
        out_specs=INNER,
        out_shape=jax.ShapeDtypeStruct((Z * CORE, BLOCK + EXTRA, HALF), BF),
        scratch_shapes=[
            pltpu.VMEM((Z * CORE * BLOCK, HALF), F32),
            pltpu.VMEM((Z * CORE, BLOCK, HALF), BF),
            pltpu.VMEM(terms.shape, BF),
            pltpu.SemaphoreType.DMA((Z,)),
            pltpu.SemaphoreType.DMA((Z,)),
        ],
        compiler_params=params(),
        cost_estimate=cheap(),
        name="pack",
    )(terms, *blocks)


def unpack_kernel(scale, in_ref, gain_ref, rows_ref, key_ref, value_ref, gains_ref):
    for which, ref in enumerate((key_ref, value_ref)):
        total = in_ref[which, :BLOCK].astype(F32)
        for z in range(1, Z):
            total = total + in_ref[z * 2 + which, :BLOCK].astype(F32)
        ref[...] = total * (gain_ref[...] * scale)
    extra = in_ref[0, BLOCK:].astype(F32)
    for at in range(1, Z * CORE):
        extra = extra + in_ref[at, BLOCK:].astype(F32)
    for line in range(2):
        gains = extra[line : line + 1] + extra[line + 2 : line + 3]
        for piece in range(2):
            lanes = gains[:, piece * 128 : (piece + 1) * 128]
            for at in range(Y * XL * XH):
                gains_ref[at, line * 2 + piece : line * 2 + piece + 1] = lanes


def unpack(scale, received, gain_rows, rows):
    def kernel(*refs):
        unpack_kernel(scale, *refs)

    return pl.pallas_call(
        kernel,
        in_specs=[INNER, INNER, ANY],
        out_specs=[INNER] * 3,
        out_shape=[
            jax.ShapeDtypeStruct((BLOCK, HALF), F32),
            jax.ShapeDtypeStruct((BLOCK, HALF), F32),
            jax.ShapeDtypeStruct((Y * XL * XH, 4, 128), F32),
        ],
        compiler_params=params(),
        cost_estimate=cheap(),
        name="unpack",
    )(received, gain_rows, rows)


def weight_rows(buf, part):
    rows = WIDE // BLOCK
    ref = buf.at[pl.ds(part * rows, rows)]
    return jnp.concatenate([ref[:, half].reshape(WIDE, HALF) for half in range(XH)], axis=1)


def rows_kernel(x_ref, gain_ref, inv_ref, keys_ref, values_ref, *rest):
    mine, theirs = rest[: len(RING)], rest[len(RING) : 2 * len(RING)]
    (out_keys_ref, out_values_ref, dx_ref, x_buf, w_buf, d_buf, inv_buf, gain_buf, out_buf, dx_buf,
     sems, small_sems, out_sems, dx_sems) = rest[2 * len(RING) :]
    core = lax.axis_index("core")
    rows = W // BLOCK

    def columns(at):
        z = lax.rem(lax.axis_index("z") + Z - at, Z)
        return pl.ds(pl.multiple_of(z * W, W), W)

    def fetch(part):
        pairs = []
        for at in range(part * WIDE // W, (part + 1) * WIDE // W):
            lanes = pl.ds(at * W, W)
            pairs.append((x_ref.at[:, columns(at)], x_buf.at[:, lanes]))
            pairs.append((gain_ref.at[:, columns(at)], gain_buf.at[:, lanes]))
            for which, refs in enumerate((mine, theirs)):
                for (distance, first, groups), ref in zip(RING, refs):
                    if distance == at:
                        block = pl.ds(at * rows + first * CORE, groups * CORE)
                        pairs.append((ref, w_buf.at[which, block]))
        return copies(pairs, sems.at[part])

    large = [fetch(0)]
    small = copies([(inv_ref, inv_buf)], small_sems)
    small.append(pick(core, keys_ref, values_ref, d_buf.at[0], small_sems.at[1]))
    small.append(pick(core, values_ref, keys_ref, d_buf.at[1], small_sems.at[2]))
    large.append(fetch(1))
    small[0].wait()
    totals = [None, None]
    for part in range(STEPS):
        for copy in large[part]:
            copy.wait()
        if part + 2 < STEPS:
            large.append(fetch(part + 2))
        lanes = slice(part * WIDE, (part + 1) * WIDE)
        normal = x_buf[:, lanes].astype(F32) * inv_buf[:, :1]
        hidden = (normal * gain_buf[:, lanes]).astype(BF)
        for which in range(2):
            weights = weight_rows(w_buf.at[which], part)
            term = jnp.dot(hidden, weights, preferred_element_type=F32)
            totals[which] = term if totals[which] is None else totals[which] + term
    for copy in small[1:]:
        copy.wait()
    sent = []
    along = None
    for which in range(2):
        out_buf[which] = totals[which].astype(BF)
        refs = (out_keys_ref, out_values_ref) if which == 0 else (out_values_ref, out_keys_ref)

        @pl.when(core == 0)
        def _():
            pltpu.make_async_copy(out_buf.at[which], refs[0], out_sems.at[which]).start()

        @pl.when(core != 0)
        def _():
            pltpu.make_async_copy(out_buf.at[which], refs[1], out_sems.at[which]).start()

        sent.append(pltpu.make_async_copy(out_buf.at[which], refs[0], out_sems.at[which]))
        term = jnp.sum(totals[which] * d_buf[which].astype(F32), axis=1, keepdims=True)
        along = term if along is None else along + term
    along = along * (1.0 / D)
    inverse = inv_buf[:, :1]
    for part in range(STEPS):
        lanes = slice(part * WIDE, (part + 1) * WIDE)
        d_hidden = None
        for which in range(2):
            term = lax.dot_general(
                d_buf[which],
                weight_rows(w_buf.at[which], part),
                (((1,), (1,)), ((), ())),
                preferred_element_type=F32,
            )
            d_hidden = term if d_hidden is None else d_hidden + term
        normal = x_buf[:, lanes].astype(F32) * inverse
        dx_buf[:, lanes] = (inverse * (d_hidden * gain_buf[:, lanes] - normal * along)).astype(BF)
        for piece in range(WIDE // W):
            at = part * (WIDE // W) + piece
            copy = pltpu.make_async_copy(
                dx_buf.at[:, pl.ds(at * W, W)], dx_ref.at[:, columns(at)], dx_sems.at[part, piece]
            )
            copy.start()
            sent.append(copy)
    for copy in sent:
        copy.wait()


def rows_pass(*inputs):
    return pl.pallas_call(
        rows_kernel,
        in_specs=[ANY] * (5 + 2 * len(RING)),
        out_specs=[ANY] * 3,
        out_shape=[
            jax.ShapeDtypeStruct((ROWS, C), BF),
            jax.ShapeDtypeStruct((ROWS, C), BF),
            jax.ShapeDtypeStruct((ROWS, D), BF),
        ],
        scratch_shapes=[
            pltpu.VMEM((ROWS, D), BF),
            pltpu.VMEM((2, D // BLOCK, XH, BLOCK, HALF), BF),
            pltpu.VMEM((2, ROWS, C), BF),
            pltpu.VMEM((ROWS, 128), F32),
            pltpu.VMEM((1, D), F32),
            pltpu.VMEM((2, ROWS, C), BF),
            pltpu.VMEM((ROWS, D), BF),
            pltpu.SemaphoreType.DMA((STEPS, 10)),
            pltpu.SemaphoreType.DMA((3,)),
            pltpu.SemaphoreType.DMA((2,)),
            pltpu.SemaphoreType.DMA((STEPS, WIDE // W)),
        ],
        compiler_params=params(),
        cost_estimate=pl.CostEstimate(
            flops=8 * ROWS * D * C, bytes_accessed=18 << 20, transcendentals=0
        ),
        name="rows_pass",
    )(*inputs)


def finish_kernel(scale, in_ref, out_ref):
    sums_of = [in_ref[at * XH] + in_ref[at * XH + 1] for at in range(Y * XL)]
    for z in range(Z):
        line, lanes = z // 2, slice(z % 2 * 64, z % 2 * 64 + 64)
        for at in range(0, Y * XL, 2):
            first, second = (sums_of[at + i][line : line + 1, lanes] for i in range(2))
            tile = jnp.concatenate([first, second], axis=1) * scale
            span = slice(z * W + at * 64, z * W + at * 64 + 128)
            out_ref[:, span] = tile


def finish(scale, gains):
    def kernel(*refs):
        finish_kernel(scale, *refs)

    return pl.pallas_call(
        kernel,
        in_specs=[INNER],
        out_specs=INNER,
        out_shape=jax.ShapeDtypeStruct((1, D), F32),
        compiler_params=params(SMALL),
        cost_estimate=cheap(),
        name="finish",
    )(gains)


def swap(a):
    return lax.ppermute(a, "core", [(0, 1), (1, 0)])


def along_z(a, step):
    return lax.ppermute(a, "z", [(i, (i + step) % Z) for i in range(Z)])


def around(own):
    up, down = [own], [own]
    for _ in range(3):
        up.append(along_z(up[-1], 1))
        down.append(along_z(down[-1], -1))
    last = [along_z(up[3][: GROUPS // 2], 1), along_z(down[3][GROUPS // 2 :], -1)]
    return up + last + down[:0:-1]


def shards(tokens, gain, w_key, w_value, d_keys, d_values):
    scale = 1.0 / math.sqrt(ROWS * Z * Y * XL * CORE * XH)
    row_gain = gain.reshape(1, D)
    block = lax.axis_index(("z", "y", "xl", "core"))
    gain_rows = lax.dynamic_slice(gain, (block * BLOCK,), (BLOCK,))
    gain_rows = jnp.broadcast_to(gain_rows[:, None], (BLOCK, HALF))

    which = lax.broadcasted_iota(jnp.int32, (Y * XL, CORE, XH, BLOCK, HALF), 1)
    sent = jnp.where(which == 0, w_key[None, None, None], w_value[None, None, None])
    plane = lax.all_to_all(
        sent.reshape(Y * XL * CORE * XH, BLOCK, HALF), ("y", "xl", "core", "xh"), 0, 0, tiled=True
    )

    inputs = (tokens, swap(tokens), d_keys, d_values, swap(d_keys), swap(d_values))
    terms, inv = gradient_terms(*inputs)
    plane = plane.reshape(GROUPS, CORE, XH, BLOCK, HALF)
    mine = around(plane)
    theirs = [swap(block) for block in mine]

    sent = pack(lax.all_to_all(terms, PLANE, 0, 0, tiled=True), mine)
    received = lax.all_to_all(sent, ("z", "core"), 0, 0, tiled=True)

    flat = [block.reshape(-1, XH, BLOCK, HALF) for block in mine + theirs]
    keys, values, d_tokens = rows_pass(tokens, row_gain, inv, d_keys, d_values, *flat)
    grad_key, grad_value, gains = unpack(scale, received, gain_rows, keys)
    gains = lax.all_to_all(gains, PLANE, 0, 0, tiled=True)
    grad_gain = finish(scale, gains).reshape(D)
    return (keys, values, d_tokens, grad_key, grad_value, grad_gain)


def solution(mesh):
    fine = Mesh(mesh.devices.reshape(Z, Y, XL, CORE, XH), AXES)
    loop = ("z", "y", "xl", "core")
    return jax.shard_map(
        shards,
        mesh=fine,
        in_specs=(
            P(AXES, None),
            P(),
            P(loop, "xh"),
            P(loop, "xh"),
            P(AXES, None),
            P(AXES, None),
        ),
        out_specs=(
            P(AXES, None),
            P(AXES, None),
            P(AXES, None),
            P(loop, "xh"),
            P(loop, "xh"),
            P(),
        ),
        check_vma=False,
    )
```
